32 devices in a mesh: dp: 4 (over z), expert: 8 (over y, x, core).
Axes of the slice: x: 2, y: 2, z: 4, core: 2. Of those that a mesh axis runs over, the one named last changes fastest.
Arguments:
- row_codes: bfloat16 [1024, 4096], P('expert', 'dp'), may hold values from -6 to 6
- scales: bfloat16 [1024, 32], P('expert', 'dp'), may hold values from 0.125 to 2
- routes: int32 [1024, 8], P('expert'), may hold values from 0 to 255, as said below
- mix_weights: float32 [1024, 8], P('expert'), may hold values from 0.05 to 1
- w_gate: bfloat16 [8, 4096, 1024], P('expert', 'dp'), may hold values from -0.09375 to 0.09375
- w_up: bfloat16 [8, 4096, 1024], P('expert', 'dp'), may hold values from -0.09375 to 0.09375
- w_down: bfloat16 [8, 1024, 4096], P('expert', None, 'dp'), may hold values from -0.1875 to 0.1875
- grad_out: bfloat16 [1024, 4096], P('expert', 'dp'), may hold values from -6 to 6
Outputs:
- mixed_out: bfloat16 [1024, 4096], P('expert', 'dp')
- grad_rows: bfloat16 [1024, 4096], P('expert', 'dp')
- grad_gate: bfloat16 [8, 4096, 1024], P('expert', 'dp')
- grad_up: bfloat16 [8, 4096, 1024], P('expert', 'dp')
- grad_down: bfloat16 [8, 1024, 4096], P('expert', None, 'dp')
The draws below stay inside these ranges and needn't reach their ends.
Inputs may be any that keep to these rules, and one draw needn't show every extreme that they name: `routes`: each row names 8 different routed experts; the ids below 8 are the experts of the window, id e held on index e of expert. In each aligned block of 128 rows (the tokens of one index of expert) no id is named by more than 8 rows, and one id below 8, the same in every block, is named by exactly 8 rows.
All inputs are finite; a program needn't handle non-finite values.
Results may differ from the reference program's by a relative error of at most 0.018.
Values may be sent and summed in bfloat16 or wider, within the bound.
No kernel may reach another device: no remote copies, remote signals or barrier semaphores. Data moves between devices by JAX's collectives and lax.ppermute only.
A program may use at most 64 MiB of HBM per device.

```python
import math
import jax
import jax.numpy as jnp
from jax import lax

D = 4096
H = 1024
ROUTED = 256
K = 8
TOK_DEV = 128
EXPERTS = 8
CAP = 8
TOKENS = 1024
FEAT_DEV = 1024


def draw_routes(key, part):
    key = jax.random.fold_in(key, 7)
    hot_key, block_key = jax.random.split(key)
    favored = jax.random.randint(hot_key, (), 0, EXPERTS).astype(jnp.int32)
    average = TOK_DEV * K // ROUTED

    def one_block(sub_key):
        perm_key, offset_key, row_key = jax.random.split(sub_key, 3)
        ordering = jax.random.permutation(perm_key, ROUTED).astype(jnp.int32)
        ordering = jnp.where(ordering == favored, ordering[0], ordering).at[0].set(favored)
        spread = jax.random.randint(offset_key, (ROUTED // 2,), 0, average + 1).astype(jnp.int32)
        spread = spread.at[0].set(average)
        counts = jnp.stack([average + spread, average - spread], axis=1).reshape(-1)
        bounds = jnp.cumsum(counts)
        position = jnp.arange(TOK_DEV * K, dtype=jnp.int32)
        slot_of = jnp.sum((position[:, None] >= bounds[None, :]).astype(jnp.int32), axis=1)
        listed = ordering[slot_of]
        layout = listed.reshape(K, TOK_DEV).T
        shuffle = jax.random.permutation(row_key, TOK_DEV)
        return layout[shuffle]
    sub_keys = jax.random.split(block_key, TOKENS // TOK_DEV)
    return jax.vmap(one_block)(sub_keys).reshape(TOKENS, K).astype(jnp.int32)


def block_scale(key, extent, shards, smallest, largest):
    level = 1.0
    for dim, parts in shards:
        draws = jax.random.uniform(jax.random.fold_in(jax.random.fold_in(key, 6), dim), (parts,), jnp.float32, smallest / len(shards), largest / len(shards))
        level = level * jnp.repeat(jnp.exp(draws), extent[dim] // parts).reshape((-1,) + (1,) * (len(extent) - 1 - dim))
    return level


def scatter_about(rng, extent, scale, limit, cuts=(), kind=jnp.bfloat16):
    result = scale * jax.random.normal(rng, extent, jnp.float32)
    if cuts:
        result = result * block_scale(rng, extent, cuts, -0.22, 0.18)
    return jnp.clip(result, -limit, limit).astype(kind)


def setup_inputs(seed: int = 0) -> dict:
    streams_of = jax.random.split(jax.random.key(seed), 9)
    return {
        "row_codes": scatter_about(streams_of[0], (TOKENS, D), 1.0, 6.0, ((0, 8), (1, 4))),
        "scales": jnp.clip(jnp.exp(math.log(2.0) - 2.7725887 * jax.random.uniform(streams_of[1], (TOKENS, D // 128), jnp.float32) ** block_scale(streams_of[1], (TOKENS, D // 128), ((0, 8), (1, 4)), -0.2, 0.2)), 0.125, 2.0).astype(jnp.bfloat16),
        "routes": draw_routes(jax.random.fold_in(streams_of[8], 71), 0),
        "mix_weights": jnp.clip(jnp.exp(math.log(1.0) - 2.9957323 * jax.random.uniform(streams_of[3], (TOKENS, K), jnp.float32) ** block_scale(streams_of[3], (TOKENS, K), ((0, 8),), -0.2, 0.2)), 0.05, 1.0),
        "w_gate": scatter_about(streams_of[4], (EXPERTS, D, H), D ** -0.5, 0.09375, ((0, 8), (1, 4))),
        "w_up": scatter_about(streams_of[5], (EXPERTS, D, H), D ** -0.5, 0.09375, ((0, 8), (1, 4))),
        "w_down": scatter_about(streams_of[6], (EXPERTS, H, D), H ** -0.5, 0.1875, ((0, 8), (2, 4))),
        "grad_out": scatter_about(streams_of[7], (TOKENS, D), 1.0, 6.0, ((0, 8), (1, 4))),
    }


def partial_sum(left, right):
    rows = left.shape[0]
    sliced = left.astype(jnp.float32).reshape(rows, -1, FEAT_DEV)
    weight = right.astype(jnp.float32).reshape(-1, FEAT_DEV, right.shape[1])
    partials = jnp.einsum("rsf,sfm->srm", sliced, weight)
    rounded = lax.optimization_barrier(partials.astype(jnp.bfloat16))
    return jnp.sum(rounded.astype(jnp.float32), axis=0)


def reference(row_codes, scales, routes, mix_weights, w_gate, w_up, w_down, grad_out):
    blocks = TOKENS // TOK_DEV
    slot_count = blocks * CAP
    flat_ids = routes.reshape(blocks, TOK_DEV * K)
    one_hot = (flat_ids[:, :, None] == jnp.arange(EXPERTS, dtype=jnp.int32)[None, None, :]).astype(jnp.int32)
    ranking = jnp.sum((jnp.cumsum(one_hot, axis=1) - one_hot) * one_hot, axis=2)
    block_idx = jnp.arange(blocks, dtype=jnp.int32)[:, None]
    target = jnp.where(flat_ids < EXPERTS, flat_ids * slot_count + block_idx * CAP + ranking, EXPERTS * slot_count)
    target = target.reshape(-1).astype(jnp.int32)
    route_ids = jnp.arange(TOKENS * K, dtype=jnp.int32)
    slot_table = jnp.full((EXPERTS * slot_count + 1,), TOKENS * K, jnp.int32).at[target].set(route_ids)
    slot_table = slot_table[:-1].reshape(EXPERTS, slot_count)
    dequant = (row_codes.astype(jnp.float32) * jnp.repeat(scales.astype(jnp.float32), 128, axis=1)).astype(jnp.bfloat16)
    padded_rows = jnp.concatenate([dequant, jnp.zeros((1, D), jnp.bfloat16)], axis=0)
    weighted = (mix_weights[:, :, None] * grad_out.astype(jnp.float32)[:, None, :]).astype(jnp.bfloat16)
    weighted = jnp.concatenate([weighted.reshape(TOKENS * K, D), jnp.zeros((1, D), jnp.bfloat16)], axis=0)

    def expert(inputs):
        gate_w, up_w, down_w, route_slot = inputs
        token_idx = jnp.where(route_slot < TOKENS * K, route_slot // K, TOKENS).astype(jnp.int32)
        expert_rows = padded_rows[token_idx]
        slot_grads = weighted[route_slot]
        gate_act = partial_sum(expert_rows, gate_w)
        up_act = partial_sum(expert_rows, up_w)
        hidden = (jax.nn.silu(gate_act) * up_act).astype(jnp.bfloat16)
        expert_out = jnp.dot(hidden, down_w, preferred_element_type=jnp.float32).astype(jnp.bfloat16)
        hidden_grad = partial_sum(slot_grads, down_w.T)
        sig_gate = jax.nn.sigmoid(gate_act)
        gate_grad = (hidden_grad * up_act * sig_gate * (1.0 + gate_act * (1.0 - sig_gate))).astype(jnp.bfloat16)
        up_grad = (hidden_grad * gate_act * sig_gate).astype(jnp.bfloat16)
        row_grad = (jnp.dot(gate_grad, gate_w.T, preferred_element_type=jnp.float32)
                    + jnp.dot(up_grad, up_w.T, preferred_element_type=jnp.float32)).astype(jnp.bfloat16)
        grad_gate = jnp.dot(expert_rows.T, gate_grad, preferred_element_type=jnp.float32).astype(jnp.bfloat16)
        grad_up = jnp.dot(expert_rows.T, up_grad, preferred_element_type=jnp.float32).astype(jnp.bfloat16)
        grad_down = jnp.dot(hidden.T, slot_grads, preferred_element_type=jnp.float32).astype(jnp.bfloat16)
        return expert_out, row_grad, grad_gate, grad_up, grad_down

    expert_outs, expert_grads, grad_gate, grad_up, grad_down = lax.map(expert, (w_gate, w_up, w_down, slot_table))
    zero_row = jnp.zeros((1, D), jnp.bfloat16)
    outs_flat = jnp.concatenate([expert_outs.reshape(EXPERTS * slot_count, D), zero_row], axis=0)
    grads_flat = jnp.concatenate([expert_grads.reshape(EXPERTS * slot_count, D), zero_row], axis=0)
    picked = outs_flat[target].reshape(TOKENS, K, D).astype(jnp.float32)
    mixed_out = jnp.sum(picked * mix_weights[:, :, None], axis=1).astype(jnp.bfloat16)
    grad_rows = jnp.sum(grads_flat[target].reshape(TOKENS, K, D).astype(jnp.float32), axis=1).astype(jnp.bfloat16)
    return mixed_out, grad_rows, grad_gate, grad_up, grad_down
```

```python
import functools

import jax
import jax.numpy as jnp
from jax import lax
from jax.experimental import pallas as pl
from jax.experimental.pallas import tpu as pltpu
from jax.sharding import PartitionSpec as P

CAP = 8
F32 = jnp.float32
BF16 = jnp.bfloat16
VMEM_SPEC = pl.BlockSpec(memory_space=pltpu.VMEM)


def dot(left, right, left_dim, right_dim):
    return lax.dot_general(
        left, right, (((left_dim,), (right_dim,)), ((), ())), preferred_element_type=F32
    )


def call(kernel, out_shape, flops=0, bytes_accessed=0, mib=24):
    many = isinstance(out_shape, (tuple, list))
    return pl.pallas_call(
        kernel,
        out_shape=out_shape,
        out_specs=[VMEM_SPEC] * len(out_shape) if many else VMEM_SPEC,
        compiler_params=pltpu.CompilerParams(vmem_limit_bytes=mib << 20),
        cost_estimate=pl.CostEstimate(
            flops=flops, bytes_accessed=bytes_accessed, transcendentals=0
        ),
    )


def route_kernel(routes_ref, mix_ref, scales_ref, codes_ref, grad_ref, send_ref, place_ref, blend_ref):
    owners = send_ref.shape[0]
    picks, tokens = routes_ref.shape
    slots = owners * CAP
    ids = lax.broadcasted_iota(jnp.int32, (owners, tokens), 0)
    match = jnp.zeros((owners, tokens), F32)
    weight = jnp.zeros((owners, tokens), F32)
    for k in range(picks):
        hit = routes_ref[k : k + 1, :] == ids
        match = jnp.where(hit, 1.0, match)
        weight = jnp.where(hit, mix_ref[k : k + 1, :], weight)
    before = (
        lax.broadcasted_iota(jnp.int32, (tokens, tokens), 0)
        < lax.broadcasted_iota(jnp.int32, (tokens, tokens), 1)
    ).astype(BF16)
    rank = dot(match.astype(BF16), before, 1, 0).astype(jnp.int32)
    rank = jnp.where(match > 0.0, rank, -1)
    position = lax.broadcasted_iota(jnp.int32, (owners, CAP, tokens), 1)
    taken = (rank[:, None, :] == position).reshape(slots, tokens)
    weights = jnp.broadcast_to(weight[:, None, :], (owners, CAP, tokens)).reshape(slots, tokens)
    blend = jnp.where(taken, weights, 0.0)
    place = jnp.where(taken, 1.0, 0.0).astype(BF16)
    place_ref[...] = place
    blend_ref[...] = blend.astype(BF16)
    slot_weight = jnp.sum(blend, axis=1, keepdims=True)
    slot_scale = dot(place, scales_ref[...], 1, 1)
    codes = dot(place, codes_ref[...], 1, 0)
    features = codes.shape[1]
    groups = scales_ref.shape[0]
    width = features // groups
    rows = jnp.concatenate(
        [codes[:, g * width : (g + 1) * width] * slot_scale[:, g : g + 1] for g in range(groups)],
        axis=1,
    )
    grads = dot(place, grad_ref[...], 1, 0) * slot_weight
    both = jnp.concatenate(
        [rows.reshape(owners, CAP, features), grads.reshape(owners, CAP, features)], axis=1
    )
    send_ref[...] = both.astype(BF16)


def split_pair(ref):
    owners, both, features = ref.shape
    wide = ref[...].astype(F32).reshape(owners, 2, CAP, features)
    return (
        wide[:, 0].reshape(owners * CAP, features).astype(BF16),
        wide[:, 1].reshape(owners * CAP, features).astype(BF16),
    )


def partial_kernel(got_ref, gate_ref, up_ref, down_ref, send_ref):
    rows, grads = split_pair(got_ref)
    owners, _, share, hidden = send_ref.shape
    send_ref[:, 0] = dot(rows, gate_ref[...], 1, 0).astype(BF16).reshape(owners, share, hidden)
    send_ref[:, 1] = dot(rows, up_ref[...], 1, 0).astype(BF16).reshape(owners, share, hidden)
    send_ref[:, 2] = dot(grads, down_ref[...], 1, 1).astype(BF16).reshape(owners, share, hidden)


def gating_kernel(got_ref, out_ref):
    gate, up, hidden_grad = (jnp.sum(got_ref[:, i].astype(F32), axis=0) for i in range(3))
    sig = jax.nn.sigmoid(gate)
    silu = gate * sig
    out_ref[0] = (silu * up).astype(BF16)
    out_ref[1] = (hidden_grad * up * sig * (1.0 + gate * (1.0 - sig))).astype(BF16)
    out_ref[2] = (hidden_grad * silu).astype(BF16)


def output_kernel(acts_ref, gate_ref, up_ref, down_ref, send_ref):
    shares, _, share, width = acts_ref.shape
    slots = shares * share
    owners, _, features = send_ref.shape
    hidden, gate_grad, up_grad = (acts_ref[:, i].reshape(slots, width) for i in range(3))
    out = dot(hidden, down_ref[...], 1, 0)
    back = dot(gate_grad, gate_ref[...], 1, 1) + dot(up_grad, up_ref[...], 1, 1)
    both = jnp.concatenate(
        [out.reshape(owners, CAP, features), back.reshape(owners, CAP, features)], axis=1
    )
    send_ref[...] = both.astype(BF16)


def weight_kernel(got_ref, acts_ref, gate_ref, up_ref, down_ref):
    rows, grads = split_pair(got_ref)
    shares, _, share, width = acts_ref.shape
    hidden, gate_grad, up_grad = (acts_ref[:, i].reshape(shares * share, width) for i in range(3))
    gate_ref[0] = dot(rows, gate_grad, 0, 0).astype(BF16)
    up_ref[0] = dot(rows, up_grad, 0, 0).astype(BF16)
    down_ref[0] = dot(hidden, grads, 0, 0).astype(BF16)


def combine_kernel(got_ref, place_ref, blend_ref, mixed_ref, rows_ref):
    outs, backs = split_pair(got_ref)
    mixed_ref[...] = dot(blend_ref[...], outs, 0, 0).astype(BF16)
    rows_ref[...] = dot(place_ref[...], backs, 0, 0).astype(BF16)


def swap(array, axis):
    return lax.all_to_all(array, axis, split_axis=0, concat_axis=0, tiled=True)


def gather_dp(array):
    return lax.all_to_all(
        jnp.broadcast_to(array[None], (lax.axis_size("dp"),) + array.shape),
        "dp",
        split_axis=0,
        concat_axis=0,
        tiled=True,
    )


def on_device(row_codes, scales, routes, mix_weights, w_gate, w_up, w_down, grad_out):
    owners = lax.axis_size("expert")
    shares = lax.axis_size("dp")
    tokens, features = row_codes.shape
    width = w_gate.shape[2]
    slots = owners * CAP
    share = slots // shares
    gate_w, up_w, down_w = w_gate[0], w_up[0], w_down[0]
    shape = jax.ShapeDtypeStruct
    one = 2 * slots * features * width
    send, place, blend = call(
        route_kernel,
        (
            shape((owners, 2 * CAP, features), BF16),
            shape((slots, tokens), BF16),
            shape((slots, tokens), BF16),
        ),
    )(routes.T, mix_weights.T, scales.T, row_codes, grad_out)
    got = swap(send, "expert")
    partials = call(partial_kernel, shape((shares, 3, share, width), BF16), 3 * one)(
        got, gate_w, up_w, down_w
    )
    summed = swap(partials, "dp")
    acts = gather_dp(call(gating_kernel, shape((3, share, width), BF16))(summed))
    back = swap(
        call(output_kernel, shape((owners, 2 * CAP, features), BF16), 3 * one)(
            acts, gate_w, up_w, down_w
        ),
        "expert",
    )
    grad_gate, grad_up, grad_down = call(
        weight_kernel,
        (
            shape((1, features, width), BF16),
            shape((1, features, width), BF16),
            shape((1, width, features), BF16),
        ),
        3 * one,
        6 * features * width,
    )(got, acts)
    mixed_out, grad_rows = call(
        combine_kernel, (shape((tokens, features), BF16), shape((tokens, features), BF16))
    )(back, place, blend)
    return mixed_out, grad_rows, grad_gate, grad_up, grad_down


def solution(mesh):
    placed = (
        P("expert", "dp"),
        P("expert", "dp"),
        P("expert", None),
        P("expert", None),
        P("expert", "dp", None),
        P("expert", "dp", None),
        P("expert", None, "dp"),
        P("expert", "dp"),
    )
    return jax.shard_map(
        on_device,
        mesh=mesh,
        in_specs=placed,
        out_specs=(
            P("expert", "dp"),
            P("expert", "dp"),
            P("expert", "dp", None),
            P("expert", "dp", None),
            P("expert", None, "dp"),
        ),
        check_vma=False,
    )
```

```python
import jax
import jax.numpy as jnp
from jax import lax
from jax.experimental import pallas as pl
from jax.experimental.pallas import tpu as pltpu
from jax.sharding import PartitionSpec as P

CAP = 8
CORES = 2
F32 = jnp.float32
BF16 = jnp.bfloat16
VMEM_SPEC = pl.BlockSpec(memory_space=pltpu.VMEM)
HBM_SPEC = pl.BlockSpec(memory_space=pltpu.HBM)


def dot(left, right, left_dim, right_dim):
    return lax.dot_general(
        left, right, (((left_dim,), (right_dim,)), ((), ())), preferred_element_type=F32
    )


def call(kernel, out_shape, in_specs=None, scratch=(), flops=0, bytes_accessed=0, mib=8):
    many = isinstance(out_shape, (tuple, list))

    def run(*args):
        return pl.pallas_call(
            kernel,
            out_shape=out_shape,
            in_specs=in_specs or [VMEM_SPEC] * len(args),
            out_specs=[VMEM_SPEC] * len(out_shape) if many else VMEM_SPEC,
            scratch_shapes=scratch,
            compiler_params=pltpu.CompilerParams(vmem_limit_bytes=mib << 20),
            cost_estimate=pl.CostEstimate(
                flops=flops, bytes_accessed=bytes_accessed, transcendentals=0
            ),
        )(*args)

    return run


def in_hbm(array):
    return pltpu.with_memory_space_constraint(array, pltpu.HBM)


def load_all(sources, targets, sems):
    copies = [
        pltpu.make_async_copy(source, target, sems.at[i])
        for i, (source, target) in enumerate(zip(sources, targets))
    ]
    for copy in copies:
        copy.start()
    return copies


def route_kernel(
    routes_hbm, mix_hbm, scales_hbm, codes_hbm, grad_hbm,
    mine_ref, theirs_ref, place_ref, blend_ref,
    routes_ref, mix_ref, scales_ref, codes_ref, grad_ref, sems,
):
    copies = load_all(
        (routes_hbm, mix_hbm, scales_hbm, codes_hbm, grad_hbm),
        (routes_ref, mix_ref, scales_ref, codes_ref, grad_ref),
        sems,
    )
    owners = CORES * mine_ref.shape[0]
    picks, tokens = routes_ref.shape
    slots = owners * CAP
    ids = lax.broadcasted_iota(jnp.int32, (owners, tokens), 0) ^ lax.axis_index("expert")
    match = jnp.zeros((owners, tokens), F32)
    weight = jnp.zeros((owners, tokens), F32)
    copies[0].wait()
    copies[1].wait()
    for k in range(picks):
        hit = routes_ref[k : k + 1, :] == ids
        match = jnp.where(hit, 1.0, match)
        weight = jnp.where(hit, mix_ref[k : k + 1, :], weight)
    before = (
        lax.broadcasted_iota(jnp.int32, (tokens, tokens), 0)
        < lax.broadcasted_iota(jnp.int32, (tokens, tokens), 1)
    ).astype(BF16)
    rank = dot(match.astype(BF16), before, 1, 0).astype(jnp.int32)
    rank = jnp.where(match > 0.0, rank, -1)
    position = lax.broadcasted_iota(jnp.int32, (owners, CAP, tokens), 1)
    taken = (rank[:, None, :] == position).reshape(slots, tokens)
    weights = jnp.broadcast_to(weight[:, None, :], (owners, CAP, tokens)).reshape(slots, tokens)
    blend = jnp.where(taken, weights, 0.0)
    place = jnp.where(taken, 1.0, 0.0).astype(BF16)
    place_ref[...] = place
    blend_ref[...] = blend.astype(BF16)
    slot_weight = jnp.sum(blend, axis=1, keepdims=True)
    copies[2].wait()
    slot_scale = dot(place, scales_ref[...], 1, 1)
    copies[3].wait()
    codes = dot(place, codes_ref[...], 1, 0)
    features = codes.shape[1]
    groups = scales_ref.shape[0]
    width = features // groups
    rows = jnp.concatenate(
        [codes[:, g * width : (g + 1) * width] * slot_scale[:, g : g + 1] for g in range(groups)],
        axis=1,
    )
    copies[4].wait()
    grads = dot(place, grad_ref[...], 1, 0) * slot_weight
    store_pairs(rows, grads, mine_ref, theirs_ref)


def store_pairs(first, second, mine_ref, theirs_ref):
    chips, _, features = mine_ref.shape
    both = jnp.concatenate(
        [
            first.reshape(chips, CORES, CAP, features),
            second.reshape(chips, CORES, CAP, features),
        ],
        axis=2,
    ).astype(BF16)
    mine_ref[...] = both[:, 0]
    theirs_ref[...] = both[:, 1]


def pack_kernel(mine_ref, got_ref, *outs):
    for k, out in enumerate(outs):
        out[0] = mine_ref[k]
        out[1] = got_ref[k]


def fetch_kernel(after_hbm, gate_hbm, up_hbm, down_hbm, gate_ref, up_ref, down_ref, sems):
    for copy in load_all((gate_hbm, up_hbm, down_hbm), (gate_ref, up_ref, down_ref), sems):
        copy.wait()


def unpack(blocks):
    count, _, features = blocks.shape
    wide = blocks.astype(F32).reshape(count, 2, CAP, features)
    return (
        wide[:, 0].reshape(count * CAP, features).astype(BF16),
        wide[:, 1].reshape(count * CAP, features).astype(BF16),
    )


def partial_kernel(*refs, shares):
    blocks_ref = refs[-1]
    sends = refs[-1 - shares - 2 : -3]
    rows_ref, grads_ref = refs[-3:-1]
    gate_ref, up_ref, down_ref = refs[-1 - shares - 5 : -1 - shares - 2]
    got = refs[: -1 - shares - 5]
    for k, ref in enumerate(got):
        blocks_ref[CORES * k : CORES * k + CORES] = ref[...]
    owners = blocks_ref.shape[0]
    step = owners // shares
    me = lax.axis_index("dp")
    rows, grads = unpack(
        jnp.concatenate([blocks_ref[pl.ds((me ^ s) * step, step)] for s in range(shares)], axis=0)
    )
    rows_ref[...] = rows
    grads_ref[...] = grads
    share = step * CAP
    for i, part in enumerate(
        (
            dot(rows, gate_ref[...], 1, 0),
            dot(rows, up_ref[...], 1, 0),
            dot(grads, down_ref[...], 1, 1),
        )
    ):
        for s, send in enumerate(sends):
            send[i] = part[s * share : (s + 1) * share].astype(BF16)


def gating_kernel(*refs):
    parts, out_ref = refs[:-1], refs[-1]
    gate, up, hidden_grad = (sum(part[i].astype(F32) for part in parts) for i in range(3))
    sig = jax.nn.sigmoid(gate)
    silu = gate * sig
    out_ref[0] = (silu * up).astype(BF16)
    out_ref[1] = (hidden_grad * up * sig * (1.0 + gate * (1.0 - sig))).astype(BF16)
    out_ref[2] = (hidden_grad * silu).astype(BF16)


def output_kernel(*refs):
    (gate_ref, up_ref, down_ref), acts = refs[:3], refs[3:-3]
    mine_ref, theirs_ref, blocks_ref = refs[-3:]
    owners, _, features = blocks_ref.shape
    step = owners // len(acts)
    hidden, gate_grad, up_grad = (jnp.concatenate([a[i] for a in acts], axis=0) for i in range(3))
    out = dot(hidden, down_ref[...], 1, 0)
    back = dot(gate_grad, gate_ref[...], 1, 1) + dot(up_grad, up_ref[...], 1, 1)
    both = jnp.concatenate(
        [out.reshape(owners, CAP, features), back.reshape(owners, CAP, features)], axis=1
    ).astype(BF16)
    me = lax.axis_index("dp")
    for s in range(len(acts)):
        blocks_ref[pl.ds((me ^ s) * step, step)] = both[s * step : (s + 1) * step]
    for k in range(owners // CORES):
        mine_ref[k] = blocks_ref[CORES * k]
        theirs_ref[k] = blocks_ref[CORES * k + 1]


def weight_kernel(*refs):
    (rows_ref, grads_ref), acts = refs[:2], refs[2:-3]
    gate_ref, up_ref, down_ref = refs[-3:]
    rows, grads = rows_ref[...], grads_ref[...]
    hidden, gate_grad, up_grad = (jnp.concatenate([a[i] for a in acts], axis=0) for i in range(3))
    gate_ref[0] = dot(rows, gate_grad, 0, 0).astype(BF16)
    up_ref[0] = dot(rows, up_grad, 0, 0).astype(BF16)
    down_ref[0] = dot(hidden, grads, 0, 0).astype(BF16)


def combine_kernel(*refs):
    got, (place_ref, blend_ref, mixed_ref, rows_ref) = refs[:-4], refs[-4:]
    outs, backs = unpack(jnp.concatenate([ref[...] for ref in got], axis=0))
    mixed_ref[...] = dot(blend_ref[...], outs, 0, 0).astype(BF16)
    rows_ref[...] = dot(place_ref[...], backs, 0, 0).astype(BF16)


def trade(array, axis, distance):
    count = lax.axis_size(axis)
    return lax.ppermute(array, axis, [(i, i ^ distance) for i in range(count)])


def swap(mine, theirs):
    chips, rows, features = mine.shape
    got = trade(theirs, "expert", 1)
    packed = call(
        pack_kernel, (jax.ShapeDtypeStruct((CORES, rows, features), BF16),) * chips
    )(mine, got)
    return [packed[0]] + [trade(packed[k], "expert", CORES * k) for k in range(1, chips)]


def on_device(row_codes, scales, routes, mix_weights, w_gate, w_up, w_down, grad_out):
    owners = lax.axis_size("expert")
    shares = lax.axis_size("dp")
    chips = owners // CORES
    tokens, features = row_codes.shape
    width = w_gate.shape[2]
    slots = owners * CAP
    share = slots // shares
    shape = jax.ShapeDtypeStruct
    one = 2 * slots * features * width
    half = shape((chips, 2 * CAP, features), BF16)
    blocks = pltpu.VMEM((owners, 2 * CAP, features), BF16)
    loads = tuple(
        in_hbm(x) for x in (routes.T, mix_weights.T, scales.T, row_codes, grad_out)
    )
    mine, theirs, place, blend = call(
        route_kernel,
        (half, half, shape((slots, tokens), BF16), shape((slots, tokens), BF16)),
        in_specs=[HBM_SPEC] * 5,
        scratch=[pltpu.VMEM(x.shape, x.dtype) for x in loads] + [pltpu.SemaphoreType.DMA((5,))],
    )(*loads)
    got = swap(mine, theirs)
    weights = tuple(in_hbm(w[0]) for w in (w_gate, w_up, w_down))
    weights = call(
        fetch_kernel,
        tuple(pltpu.VMEM(w.shape, w.dtype) for w in weights),
        in_specs=[HBM_SPEC] * 4,
        scratch=[pltpu.SemaphoreType.DMA((3,))],
        bytes_accessed=6 * features * width,
    )(got[0], *weights)
    *partials, rows, grads = call(
        lambda *refs: partial_kernel(*refs, shares=shares),
        (shape((3, share, width), BF16),) * shares + (shape((slots, features), BF16),) * 2,
        scratch=[blocks],
        flops=3 * one,
    )(*got, *weights)
    summed = [partials[0]] + [trade(partials[s], "dp", s) for s in range(1, shares)]
    act = call(gating_kernel, shape((3, share, width), BF16))(*summed)
    acts = [act] + [trade(act, "dp", s) for s in range(1, shares)]
    back = swap(
        *call(output_kernel, (half, half), scratch=[blocks], flops=3 * one)(*weights, *acts)
    )
    grad_gate, grad_up, grad_down = call(
        weight_kernel,
        (
            shape((1, features, width), BF16),
            shape((1, features, width), BF16),
            shape((1, width, features), BF16),
        ),
        flops=3 * one,
        bytes_accessed=6 * features * width,
        mib=16,
    )(rows, grads, *acts)
    mixed_out, grad_rows = call(
        combine_kernel, (shape((tokens, features), BF16), shape((tokens, features), BF16))
    )(*back, place, blend)
    return mixed_out, grad_rows, grad_gate, grad_up, grad_down


def solution(mesh):
    placed = (
        P("expert", "dp"),
        P("expert", "dp"),
        P("expert", None),
        P("expert", None),
        P("expert", "dp", None),
        P("expert", "dp", None),
        P("expert", None, "dp"),
        P("expert", "dp"),
    )
    return jax.shard_map(
        on_device,
        mesh=mesh,
        in_specs=placed,
        out_specs=(
            P("expert", "dp"),
            P("expert", "dp"),
            P("expert", "dp", None),
            P("expert", "dp", None),
            P("expert", None, "dp"),
        ),
        check_vma=False,
    )
```

```python
import jax
import jax.numpy as jnp
from jax import lax
from jax.experimental import pallas as pl
from jax.experimental.pallas import tpu as pltpu
from jax.sharding import PartitionSpec as P

CAP = 8
CORES = 2
TILE = 256
F32 = jnp.float32
BF16 = jnp.bfloat16
VMEM_SPEC = pl.BlockSpec(memory_space=pltpu.VMEM)
HBM_SPEC = pl.BlockSpec(memory_space=pltpu.HBM)


def dot(left, right, left_dim, right_dim):
    return lax.dot_general(
        left, right, (((left_dim,), (right_dim,)), ((), ())), preferred_element_type=F32
    )


def call(
    kernel, out_shape, in_specs=None, out_specs=None, scratch=(), flops=0, bytes_accessed=0, mib=8
):
    many = isinstance(out_shape, (tuple, list))

    def run(*args):
        return pl.pallas_call(
            kernel,
            out_shape=out_shape,
            in_specs=in_specs or [VMEM_SPEC] * len(args),
            out_specs=out_specs or ([VMEM_SPEC] * len(out_shape) if many else VMEM_SPEC),
            scratch_shapes=scratch,
            compiler_params=pltpu.CompilerParams(vmem_limit_bytes=mib << 20),
            cost_estimate=pl.CostEstimate(
                flops=flops, bytes_accessed=bytes_accessed, transcendentals=0
            ),
        )(*args)

    return run


def in_hbm(array):
    return pltpu.with_memory_space_constraint(array, pltpu.HBM)


def load_all(sources, targets, sems):
    copies = [
        pltpu.make_async_copy(source, target, sems.at[i])
        for i, (source, target) in enumerate(zip(sources, targets))
    ]
    for copy in copies:
        copy.start()
    return copies


def route_kernel(
    routes_hbm, mix_hbm, scales_hbm, codes_hbm, grad_hbm,
    mine_ref, theirs_ref, place_ref, blend_ref,
    routes_ref, mix_ref, scales_ref, codes_ref, grad_ref, sems,
):
    copies = load_all(
        (routes_hbm, mix_hbm, scales_hbm, codes_hbm, grad_hbm),
        (routes_ref, mix_ref, scales_ref, codes_ref, grad_ref),
        sems,
    )
    owners = CORES * mine_ref.shape[0]
    picks, tokens = routes_ref.shape
    slots = owners * CAP
    ids = lax.broadcasted_iota(jnp.int32, (owners, tokens), 0) ^ lax.axis_index("expert")
    match = jnp.zeros((owners, tokens), F32)
    weight = jnp.zeros((owners, tokens), F32)
    copies[0].wait()
    copies[1].wait()
    for k in range(picks):
        hit = routes_ref[k : k + 1, :] == ids
        match = jnp.where(hit, 1.0, match)
        weight = jnp.where(hit, mix_ref[k : k + 1, :], weight)
    before = (
        lax.broadcasted_iota(jnp.int32, (tokens, tokens), 0)
        < lax.broadcasted_iota(jnp.int32, (tokens, tokens), 1)
    ).astype(BF16)
    rank = dot(match.astype(BF16), before, 1, 0).astype(jnp.int32)
    rank = jnp.where(match > 0.0, rank, -1)
    position = lax.broadcasted_iota(jnp.int32, (owners, CAP, tokens), 1)
    taken = (rank[:, None, :] == position).reshape(slots, tokens)
    weights = jnp.broadcast_to(weight[:, None, :], (owners, CAP, tokens)).reshape(slots, tokens)
    blend = jnp.where(taken, weights, 0.0)
    place = jnp.where(taken, 1.0, 0.0).astype(BF16)
    place_ref[...] = place
    blend_ref[...] = blend.astype(BF16)
    slot_weight = jnp.sum(blend, axis=1, keepdims=True)
    copies[2].wait()
    slot_scale = dot(place, scales_ref[...], 1, 1)
    copies[3].wait()
    codes = dot(place, codes_ref[...], 1, 0)
    features = codes.shape[1]
    groups = scales_ref.shape[0]
    width = features // groups
    rows = jnp.concatenate(
        [codes[:, g * width : (g + 1) * width] * slot_scale[:, g : g + 1] for g in range(groups)],
        axis=1,
    )
    copies[4].wait()
    grads = dot(place, grad_ref[...], 1, 0) * slot_weight
    store_pairs(rows, grads, mine_ref, theirs_ref)


def store_pairs(first, second, mine_ref, theirs_ref):
    chips, _, features = mine_ref.shape
    both = jnp.concatenate(
        [
            first.reshape(chips, CORES, CAP, features),
            second.reshape(chips, CORES, CAP, features),
        ],
        axis=2,
    ).astype(BF16)
    mine_ref[...] = both[:, 0]
    theirs_ref[...] = both[:, 1]


def pack_kernel(mine_ref, got_ref, *outs):
    for k, out in enumerate(outs):
        out[0] = mine_ref[k]
        out[1] = got_ref[k]


def fetch_kernel(after_hbm, gate_hbm, up_hbm, down_hbm, gate_ref, up_ref, down_ref, sems):
    for copy in load_all((gate_hbm, up_hbm, down_hbm), (gate_ref, up_ref, down_ref), sems):
        copy.wait()


def unpack(blocks):
    count, _, features = blocks.shape
    wide = blocks.astype(F32).reshape(count, 2, CAP, features)
    return (
        wide[:, 0].reshape(count * CAP, features).astype(BF16),
        wide[:, 1].reshape(count * CAP, features).astype(BF16),
    )


def partial_kernel(*refs, shares):
    blocks_ref = refs[-1]
    sends = refs[-1 - shares - 2 : -3]
    rows_ref, grads_ref = refs[-3:-1]
    gate_ref, up_ref, down_ref = refs[-1 - shares - 5 : -1 - shares - 2]
    got = sort_back(refs[: -1 - shares - 5])
    for k, ref in enumerate(got):
        blocks_ref[CORES * k : CORES * k + CORES] = ref[...]
    owners = blocks_ref.shape[0]
    step = owners // shares
    me = lax.axis_index("dp")
    rows, grads = unpack(
        jnp.concatenate([blocks_ref[pl.ds((me ^ s) * step, step)] for s in range(shares)], axis=0)
    )
    rows_ref[...] = rows
    grads_ref[...] = grads
    share = step * CAP
    for i, part in enumerate(
        (
            dot(rows, gate_ref[...], 1, 0),
            dot(rows, up_ref[...], 1, 0),
            dot(grads, down_ref[...], 1, 1),
        )
    ):
        for s, send in enumerate(sends):
            send[i] = part[s * share : (s + 1) * share].astype(BF16)


def gating_kernel(*refs):
    parts, out_ref = refs[:-1], refs[-1]
    gate, up, hidden_grad = (sum(part[i].astype(F32) for part in parts) for i in range(3))
    sig = jax.nn.sigmoid(gate)
    silu = gate * sig
    out_ref[0] = (silu * up).astype(BF16)
    out_ref[1] = (hidden_grad * up * sig * (1.0 + gate * (1.0 - sig))).astype(BF16)
    out_ref[2] = (hidden_grad * silu).astype(BF16)


def output_kernel(*refs):
    (gate_ref, up_ref, down_ref), acts = refs[:3], sort_back(refs[3:-3])
    mine_ref, theirs_ref, blocks_ref = refs[-3:]
    owners, _, features = blocks_ref.shape
    step = owners // len(acts)
    hidden, gate_grad, up_grad = (jnp.concatenate([a[i] for a in acts], axis=0) for i in range(3))
    out = dot(hidden, down_ref[...], 1, 0)
    back = dot(gate_grad, gate_ref[...], 1, 1) + dot(up_grad, up_ref[...], 1, 1)
    both = jnp.concatenate(
        [out.reshape(owners, CAP, features), back.reshape(owners, CAP, features)], axis=1
    ).astype(BF16)
    me = lax.axis_index("dp")
    for s in range(len(acts)):
        blocks_ref[pl.ds((me ^ s) * step, step)] = both[s * step : (s + 1) * step]
    for k in range(owners // CORES):
        mine_ref[k] = blocks_ref[CORES * k]
        theirs_ref[k] = blocks_ref[CORES * k + 1]


def weight_kernel(*refs):
    (rows_ref, grads_ref), acts = refs[:2], sort_back(refs[2:-7])
    gate_hbm, up_hbm, down_hbm, gate_ref, up_ref, down_ref, sems = refs[-7:]
    rows, grads = rows_ref[...], grads_ref[...]
    hidden, gate_grad, up_grad = (jnp.concatenate([a[i] for a in acts], axis=0) for i in range(3))
    copies = []
    for i, (left, right, out_ref, out_hbm) in enumerate(
        (
            (rows, gate_grad, gate_ref, gate_hbm),
            (rows, up_grad, up_ref, up_hbm),
            (hidden, grads, down_ref, down_hbm),
        )
    ):
        count = out_ref.shape[0] // TILE
        for j in range(count):
            part = slice(j * TILE, (j + 1) * TILE)
            out_ref[part] = dot(left[:, part], right, 0, 0).astype(BF16)
            copy = pltpu.make_async_copy(out_ref.at[part], out_hbm.at[0, part], sems.at[i, j])
            copy.start()
            copies.append(copy)
    for copy in copies:
        copy.wait()


def combine_kernel(*refs):
    got, (place_ref, blend_ref, mixed_ref, rows_ref) = sort_back(refs[:-4]), refs[-4:]
    outs, backs = unpack(jnp.concatenate([ref[...] for ref in got], axis=0))
    mixed_ref[...] = dot(blend_ref[...], outs, 0, 0).astype(BF16)
    rows_ref[...] = dot(place_ref[...], backs, 0, 0).astype(BF16)


def most_bits_first(count):
    return sorted(range(count), key=lambda k: (k > 0, -k.bit_count(), k))


def sort_back(refs):
    order = most_bits_first(len(refs))
    return [refs[order.index(k)] for k in range(len(refs))]


def trade(array, axis, distance):
    count = lax.axis_size(axis)
    return lax.ppermute(array, axis, [(i, i ^ distance) for i in range(count)])


def swap(mine, theirs):
    chips, rows, features = mine.shape
    got = trade(theirs, "expert", 1)
    packed = call(
        pack_kernel, (jax.ShapeDtypeStruct((CORES, rows, features), BF16),) * chips
    )(mine, got)
    return [trade(packed[k], "expert", CORES * k) if k else packed[0] for k in most_bits_first(chips)]


def on_device(row_codes, scales, routes, mix_weights, w_gate, w_up, w_down, grad_out):
    owners = lax.axis_size("expert")
    shares = lax.axis_size("dp")
    chips = owners // CORES
    tokens, features = row_codes.shape
    width = w_gate.shape[2]
    slots = owners * CAP
    share = slots // shares
    shape = jax.ShapeDtypeStruct
    one = 2 * slots * features * width
    half = shape((chips, 2 * CAP, features), BF16)
    blocks = pltpu.VMEM((owners, 2 * CAP, features), BF16)
    loads = tuple(
        in_hbm(x) for x in (routes.T, mix_weights.T, scales.T, row_codes, grad_out)
    )
    mine, theirs, place, blend = call(
        route_kernel,
        (half, half, shape((slots, tokens), BF16), shape((slots, tokens), BF16)),
        in_specs=[HBM_SPEC] * 5,
        scratch=[pltpu.VMEM(x.shape, x.dtype) for x in loads] + [pltpu.SemaphoreType.DMA((5,))],
    )(*loads)
    got = swap(mine, theirs)
    weights = tuple(in_hbm(w[0]) for w in (w_gate, w_up, w_down))
    weights = call(
        fetch_kernel,
        tuple(pltpu.VMEM(w.shape, w.dtype) for w in weights),
        in_specs=[HBM_SPEC] * 4,
        scratch=[pltpu.SemaphoreType.DMA((3,))],
        bytes_accessed=6 * features * width,
    )(got[0], *weights)
    *partials, rows, grads = call(
        lambda *refs: partial_kernel(*refs, shares=shares),
        (shape((3, share, width), BF16),) * shares + (shape((slots, features), BF16),) * 2,
        scratch=[blocks],
        flops=3 * one,
    )(*got, *weights)
    summed = [trade(partials[s], "dp", s) if s else partials[0] for s in range(shares)]
    act = call(gating_kernel, shape((3, share, width), BF16))(*summed)
    acts = [trade(act, "dp", s) if s else act for s in most_bits_first(shares)]
    back = swap(
        *call(output_kernel, (half, half), scratch=[blocks], flops=3 * one)(*weights, *acts),
    )
    grad_gate, grad_up, grad_down = call(
        weight_kernel,
        (
            shape((1, features, width), BF16),
            shape((1, features, width), BF16),
            shape((1, width, features), BF16),
        ),
        out_specs=[HBM_SPEC] * 3,
        scratch=[
            pltpu.VMEM((features, width), BF16),
            pltpu.VMEM((features, width), BF16),
            pltpu.VMEM((width, features), BF16),
            pltpu.SemaphoreType.DMA((3, max(features, width) // TILE)),
        ],
        flops=3 * one,
        bytes_accessed=6 * features * width,
        mib=16,
    )(rows, grads, *acts)
    mixed_out, grad_rows = call(
        combine_kernel, (shape((tokens, features), BF16), shape((tokens, features), BF16))
    )(*back, place, blend)
    return mixed_out, grad_rows, grad_gate, grad_up, grad_down


def solution(mesh):
    placed = (
        P("expert", "dp"),
        P("expert", "dp"),
        P("expert", None),
        P("expert", None),
        P("expert", "dp", None),
        P("expert", "dp", None),
        P("expert", None, "dp"),
        P("expert", "dp"),
    )
    return jax.shard_map(
        on_device,
        mesh=mesh,
        in_specs=placed,
        out_specs=(
            P("expert", "dp"),
            P("expert", "dp"),
            P("expert", "dp", None),
            P("expert", "dp", None),
            P("expert", None, "dp"),
        ),
        check_vma=False,
    )
```

```python
import jax
import jax.numpy as jnp
from jax import lax
from jax.experimental import pallas as pl
from jax.experimental.pallas import tpu as pltpu
from jax.sharding import PartitionSpec as P

CAP = 8
CORES = 2
TILE = 256
F32 = jnp.float32
BF16 = jnp.bfloat16
VMEM_SPEC = pl.BlockSpec(memory_space=pltpu.VMEM)
HBM_SPEC = pl.BlockSpec(memory_space=pltpu.HBM)


def dot(left, right, left_dim, right_dim):
    return lax.dot_general(
        left, right, (((left_dim,), (right_dim,)), ((), ())), preferred_element_type=F32
    )


def call(
    kernel, out_shape, in_specs=None, out_specs=None, scratch=(), flops=0, bytes_accessed=0, mib=8
):
    many = isinstance(out_shape, (tuple, list))

    def run(*args):
        return pl.pallas_call(
            kernel,
            out_shape=out_shape,
            in_specs=in_specs or [VMEM_SPEC] * len(args),
            out_specs=out_specs or ([VMEM_SPEC] * len(out_shape) if many else VMEM_SPEC),
            scratch_shapes=scratch,
            compiler_params=pltpu.CompilerParams(vmem_limit_bytes=mib << 20),
            cost_estimate=pl.CostEstimate(
                flops=flops, bytes_accessed=bytes_accessed, transcendentals=0
            ),
        )(*args)

    return run


def in_hbm(array):
    return pltpu.with_memory_space_constraint(array, pltpu.HBM)


def distances(shares, core):
    return [0] + (list(range(1, shares)) if core == 0 else list(range(shares - 1, 0, -1)))


def peer(shares, s):
    near, far = distances(shares, 0)[s], distances(shares, 1)[s]
    core = lax.rem(lax.axis_index("expert"), CORES)
    return lax.axis_index("dp") ^ jnp.where(core == 0, near, far)


def load_all(sources, targets, sems):
    copies = [
        pltpu.make_async_copy(source, target, sems.at[i])
        for i, (source, target) in enumerate(zip(sources, targets))
    ]
    for copy in copies:
        copy.start()
    return copies


def route_kernel(
    routes_hbm, mix_hbm, scales_hbm, codes_hbm, grad_hbm,
    mine_ref, theirs_ref, place_ref, blend_ref,
    routes_ref, mix_ref, scales_ref, codes_ref, grad_ref, sems,
):
    copies = load_all(
        (routes_hbm, mix_hbm, scales_hbm, codes_hbm, grad_hbm),
        (routes_ref, mix_ref, scales_ref, codes_ref, grad_ref),
        sems,
    )
    owners = CORES * mine_ref.shape[0]
    picks, tokens = routes_ref.shape
    slots = owners * CAP
    ids = lax.broadcasted_iota(jnp.int32, (owners, tokens), 0) ^ lax.axis_index("expert")
    match = jnp.zeros((owners, tokens), F32)
    weight = jnp.zeros((owners, tokens), F32)
    copies[0].wait()
    copies[1].wait()
    for k in range(picks):
        hit = routes_ref[k : k + 1, :] == ids
        match = jnp.where(hit, 1.0, match)
        weight = jnp.where(hit, mix_ref[k : k + 1, :], weight)
    before = (
        lax.broadcasted_iota(jnp.int32, (tokens, tokens), 0)
        < lax.broadcasted_iota(jnp.int32, (tokens, tokens), 1)
    ).astype(BF16)
    rank = dot(match.astype(BF16), before, 1, 0).astype(jnp.int32)
    rank = jnp.where(match > 0.0, rank, -1)
    position = lax.broadcasted_iota(jnp.int32, (owners, CAP, tokens), 1)
    taken = (rank[:, None, :] == position).reshape(slots, tokens)
    weights = jnp.broadcast_to(weight[:, None, :], (owners, CAP, tokens)).reshape(slots, tokens)
    blend = jnp.where(taken, weights, 0.0)
    place = jnp.where(taken, 1.0, 0.0).astype(BF16)
    place_ref[...] = place
    blend_ref[...] = blend.astype(BF16)
    slot_weight = jnp.sum(blend, axis=1, keepdims=True)
    copies[2].wait()
    slot_scale = dot(place, scales_ref[...], 1, 1)
    copies[3].wait()
    codes = dot(place, codes_ref[...], 1, 0)
    features = codes.shape[1]
    groups = scales_ref.shape[0]
    width = features // groups
    rows = jnp.concatenate(
        [codes[:, g * width : (g + 1) * width] * slot_scale[:, g : g + 1] for g in range(groups)],
        axis=1,
    )
    copies[4].wait()
    grads = dot(place, grad_ref[...], 1, 0) * slot_weight
    store_pairs(rows, grads, mine_ref, theirs_ref)


def store_pairs(first, second, mine_ref, theirs_ref):
    chips, _, features = mine_ref.shape
    both = jnp.concatenate(
        [
            first.reshape(chips, CORES, CAP, features),
            second.reshape(chips, CORES, CAP, features),
        ],
        axis=2,
    ).astype(BF16)
    mine_ref[...] = both[:, 0]
    theirs_ref[...] = both[:, 1]


def pack_kernel(mine_ref, got_ref, *outs):
    for k, out in enumerate(outs):
        out[0] = mine_ref[k]
        out[1] = got_ref[k]


def fetch_kernel(
    after_hbm, gate_hbm, up_hbm, down_hbm, gate_ref, up_ref, down_ref, flipped_ref, sems
):
    copies = load_all((down_hbm, gate_hbm, up_hbm), (down_ref, gate_ref, up_ref), sems)
    copies[0].wait()
    flipped_ref[...] = down_ref[...].T
    copies[1].wait()
    copies[2].wait()


def flip_kernel(after_hbm, gate_ref, up_ref, gate_out, up_out):
    gate_out[...] = gate_ref[...].T
    up_out[...] = up_ref[...].T


def unpack(blocks):
    count, _, features = blocks.shape
    wide = blocks.astype(F32).reshape(count, 2, CAP, features)
    return (
        wide[:, 0].reshape(count * CAP, features).astype(BF16),
        wide[:, 1].reshape(count * CAP, features).astype(BF16),
    )


def partial_kernel(*refs, shares):
    blocks_ref = refs[-1]
    sends = refs[-1 - shares - 2 : -3]
    rows_ref, grads_ref = refs[-3:-1]
    gate_ref, up_ref, down_ref = refs[-1 - shares - 5 : -1 - shares - 2]
    got = sort_back(refs[: -1 - shares - 5])
    for k, ref in enumerate(got):
        blocks_ref[CORES * k : CORES * k + CORES] = ref[...]
    owners = blocks_ref.shape[0]
    step = owners // shares
    rows, grads = unpack(
        jnp.concatenate([blocks_ref[pl.ds(peer(shares, s) * step, step)] for s in range(shares)], axis=0)
    )
    rows_ref[...] = rows
    grads_ref[...] = grads
    share = step * CAP
    for i, part in enumerate(
        (
            dot(rows, gate_ref[...], 1, 0),
            dot(rows, up_ref[...], 1, 0),
            dot(grads, down_ref[...], 1, 0),
        )
    ):
        for s, send in enumerate(sends):
            send[i] = part[s * share : (s + 1) * share].astype(BF16)


def gating_kernel(*refs):
    parts, out_ref = refs[:-1], refs[-1]
    gate, up, hidden_grad = (sum(part[i].astype(F32) for part in parts) for i in range(3))
    sig = jax.nn.sigmoid(gate)
    silu = gate * sig
    out_ref[0] = (silu * up).astype(BF16)
    out_ref[1] = (hidden_grad * up * sig * (1.0 + gate * (1.0 - sig))).astype(BF16)
    out_ref[2] = (hidden_grad * silu).astype(BF16)


def output_kernel(*refs):
    (gate_ref, up_ref, down_ref), acts = refs[:3], sort_back(refs[3:-3])
    mine_ref, theirs_ref, blocks_ref = refs[-3:]
    owners, _, features = blocks_ref.shape
    step = owners // len(acts)
    hidden, gate_grad, up_grad = (jnp.concatenate([a[i] for a in acts], axis=0) for i in range(3))
    out = dot(hidden, down_ref[...], 1, 0)
    back = dot(gate_grad, gate_ref[...], 1, 0) + dot(up_grad, up_ref[...], 1, 0)
    both = jnp.concatenate(
        [out.reshape(owners, CAP, features), back.reshape(owners, CAP, features)], axis=1
    ).astype(BF16)
    shares = len(acts)
    for s in range(shares):
        blocks_ref[pl.ds(peer(shares, s) * step, step)] = both[s * step : (s + 1) * step]
    for k in range(owners // CORES):
        mine_ref[k] = blocks_ref[CORES * k]
        theirs_ref[k] = blocks_ref[CORES * k + 1]


def weight_kernel(*refs):
    (rows_ref, grads_ref), acts = refs[:2], sort_back(refs[2:-7])
    gate_hbm, up_hbm, down_hbm, gate_ref, up_ref, down_ref, sems = refs[-7:]
    rows, grads = rows_ref[...], grads_ref[...]
    hidden, gate_grad, up_grad = (jnp.concatenate([a[i] for a in acts], axis=0) for i in range(3))
    copies = []
    for i, (left, right, out_ref, out_hbm) in enumerate(
        (
            (rows, gate_grad, gate_ref, gate_hbm),
            (rows, up_grad, up_ref, up_hbm),
            (hidden, grads, down_ref, down_hbm),
        )
    ):
        count = out_ref.shape[0] // TILE
        for j in range(count):
            part = slice(j * TILE, (j + 1) * TILE)
            out_ref[part] = dot(left[:, part], right, 0, 0).astype(BF16)
            copy = pltpu.make_async_copy(out_ref.at[part], out_hbm.at[0, part], sems.at[i, j])
            copy.start()
            copies.append(copy)
    for copy in copies:
        copy.wait()


def combine_kernel(*refs):
    got, (place_ref, blend_ref, mixed_ref, rows_ref) = sort_back(refs[:-4]), refs[-4:]
    outs, backs = unpack(jnp.concatenate([ref[...] for ref in got], axis=0))
    mixed_ref[...] = dot(blend_ref[...], outs, 0, 0).astype(BF16)
    rows_ref[...] = dot(place_ref[...], backs, 0, 0).astype(BF16)


def most_bits_first(count):
    return sorted(range(count), key=lambda k: (k > 0, -k.bit_count(), k))


def sort_back(refs):
    order = most_bits_first(len(refs))
    return [refs[order.index(k)] for k in range(len(refs))]


def trade(array, axis, distance):
    count = lax.axis_size(axis)
    return lax.ppermute(array, axis, [(i, i ^ distance) for i in range(count)])


def trade_dp(array, s):
    shares, owners = lax.axis_size("dp"), lax.axis_size("expert")
    pairs = [
        (d * owners + e, (d ^ distances(shares, e % CORES)[s]) * owners + e)
        for d in range(shares)
        for e in range(owners)
    ]
    return lax.ppermute(array, ("dp", "expert"), pairs)


def swap(mine, theirs):
    chips, rows, features = mine.shape
    got = trade(theirs, "expert", 1)
    packed = call(
        pack_kernel, (jax.ShapeDtypeStruct((CORES, rows, features), BF16),) * chips
    )(mine, got)
    return [trade(packed[k], "expert", CORES * k) if k else packed[0] for k in most_bits_first(chips)]


def on_device(row_codes, scales, routes, mix_weights, w_gate, w_up, w_down, grad_out):
    owners = lax.axis_size("expert")
    shares = lax.axis_size("dp")
    chips = owners // CORES
    tokens, features = row_codes.shape
    width = w_gate.shape[2]
    slots = owners * CAP
    share = slots // shares
    shape = jax.ShapeDtypeStruct
    one = 2 * slots * features * width
    half = shape((chips, 2 * CAP, features), BF16)
    blocks = pltpu.VMEM((owners, 2 * CAP, features), BF16)
    loads = tuple(
        in_hbm(x) for x in (routes.T, mix_weights.T, scales.T, row_codes, grad_out)
    )
    mine, theirs, place, blend = call(
        route_kernel,
        (half, half, shape((slots, tokens), BF16), shape((slots, tokens), BF16)),
        in_specs=[HBM_SPEC] * 5,
        scratch=[pltpu.VMEM(x.shape, x.dtype) for x in loads] + [pltpu.SemaphoreType.DMA((5,))],
    )(*loads)
    got = swap(mine, theirs)
    weights = tuple(in_hbm(w[0]) for w in (w_gate, w_up, w_down))
    weights = call(
        fetch_kernel,
        tuple(pltpu.VMEM(w.shape, w.dtype) for w in weights)
        + (pltpu.VMEM((features, width), BF16),),
        in_specs=[HBM_SPEC] * 4,
        scratch=[pltpu.SemaphoreType.DMA((3,))],
        bytes_accessed=6 * features * width,
    )(got[0], *weights)
    *partials, rows, grads = call(
        lambda *refs: partial_kernel(*refs, shares=shares),
        (shape((3, share, width), BF16),) * shares + (shape((slots, features), BF16),) * 2,
        scratch=[blocks],
        flops=3 * one,
    )(*got, *weights[:2], weights[3])
    gate_w, up_w, down_w, _ = weights
    flipped = call(
        flip_kernel,
        (pltpu.VMEM((width, features), BF16),) * 2,
        in_specs=[HBM_SPEC, VMEM_SPEC, VMEM_SPEC],
        bytes_accessed=16 * features * width,
    )(partials[0], gate_w, up_w)
    summed = [trade_dp(partials[s], s) if s else partials[0] for s in range(shares)]
    act = call(gating_kernel, shape((3, share, width), BF16))(*summed)
    acts = [trade_dp(act, s) if s else act for s in most_bits_first(shares)]
    back = swap(
        *call(output_kernel, (half, half), scratch=[blocks], flops=3 * one)(*flipped, down_w, *acts),
    )
    grad_gate, grad_up, grad_down = call(
        weight_kernel,
        (
            shape((1, features, width), BF16),
            shape((1, features, width), BF16),
            shape((1, width, features), BF16),
        ),
        out_specs=[HBM_SPEC] * 3,
        scratch=[
            pltpu.VMEM((features, width), BF16),
            pltpu.VMEM((features, width), BF16),
            pltpu.VMEM((width, features), BF16),
            pltpu.SemaphoreType.DMA((3, max(features, width) // TILE)),
        ],
        flops=3 * one,
        bytes_accessed=6 * features * width,
        mib=16,
    )(rows, grads, *acts)
    mixed_out, grad_rows = call(
        combine_kernel, (shape((tokens, features), BF16), shape((tokens, features), BF16))
    )(*back, place, blend)
    return mixed_out, grad_rows, grad_gate, grad_up, grad_down


def solution(mesh):
    placed = (
        P("expert", "dp"),
        P("expert", "dp"),
        P("expert", None),
        P("expert", None),
        P("expert", "dp", None),
        P("expert", "dp", None),
        P("expert", None, "dp"),
        P("expert", "dp"),
    )
    return jax.shard_map(
        on_device,
        mesh=mesh,
        in_specs=placed,
        out_specs=(
            P("expert", "dp"),
            P("expert", "dp"),
            P("expert", "dp", None),
            P("expert", "dp", None),
            P("expert", None, "dp"),
        ),
        check_vma=False,
    )
```

```python
import jax
import jax.numpy as jnp
from jax import lax
from jax.experimental import pallas as pl
from jax.experimental.pallas import tpu as pltpu
from jax.sharding import PartitionSpec as P

CAP = 8
CORES = 2
TILE = 256
EARLY = 2
F32 = jnp.float32
BF16 = jnp.bfloat16
VMEM_SPEC = pl.BlockSpec(memory_space=pltpu.VMEM)
HBM_SPEC = pl.BlockSpec(memory_space=pltpu.HBM)


def dot(left, right, left_dim, right_dim):
    return lax.dot_general(
        left, right, (((left_dim,), (right_dim,)), ((), ())), preferred_element_type=F32
    )


def call(
    kernel, out_shape, in_specs=None, out_specs=None, scratch=(), flops=0, bytes_accessed=0, mib=8,
    aliases=None,
):
    many = isinstance(out_shape, (tuple, list))

    def run(*args):
        return pl.pallas_call(
            kernel,
            out_shape=out_shape,
            in_specs=in_specs or [VMEM_SPEC] * len(args),
            out_specs=out_specs or ([VMEM_SPEC] * len(out_shape) if many else VMEM_SPEC),
            scratch_shapes=scratch,
            input_output_aliases=aliases or {},
            compiler_params=pltpu.CompilerParams(vmem_limit_bytes=mib << 20),
            cost_estimate=pl.CostEstimate(
                flops=flops, bytes_accessed=bytes_accessed, transcendentals=0
            ),
        )(*args)

    return run


def in_hbm(array):
    return pltpu.with_memory_space_constraint(array, pltpu.HBM)


def distances(shares, core):
    return [0] + (list(range(1, shares)) if core == 0 else list(range(shares - 1, 0, -1)))


def peer(shares, s):
    near, far = distances(shares, 0)[s], distances(shares, 1)[s]
    core = lax.rem(lax.axis_index("expert"), CORES)
    return lax.axis_index("dp") ^ jnp.where(core == 0, near, far)


def load_all(sources, targets, sems):
    copies = [
        pltpu.make_async_copy(source, target, sems.at[i])
        for i, (source, target) in enumerate(zip(sources, targets))
    ]
    for copy in copies:
        copy.start()
    return copies


def route_kernel(
    routes_hbm, mix_hbm, scales_hbm, codes_hbm, grad_hbm,
    mine_ref, theirs_ref, place_ref, blend_ref,
    routes_ref, mix_ref, scales_ref, codes_ref, grad_ref, sems,
):
    copies = load_all(
        (routes_hbm, mix_hbm, scales_hbm, codes_hbm, grad_hbm),
        (routes_ref, mix_ref, scales_ref, codes_ref, grad_ref),
        sems,
    )
    owners = CORES * mine_ref.shape[0]
    picks, tokens = routes_ref.shape
    slots = owners * CAP
    ids = lax.broadcasted_iota(jnp.int32, (owners, tokens), 0) ^ lax.axis_index("expert")
    match = jnp.zeros((owners, tokens), F32)
    weight = jnp.zeros((owners, tokens), F32)
    copies[0].wait()
    copies[1].wait()
    for k in range(picks):
        hit = routes_ref[k : k + 1, :] == ids
        match = jnp.where(hit, 1.0, match)
        weight = jnp.where(hit, mix_ref[k : k + 1, :], weight)
    before = (
        lax.broadcasted_iota(jnp.int32, (tokens, tokens), 0)
        < lax.broadcasted_iota(jnp.int32, (tokens, tokens), 1)
    ).astype(BF16)
    rank = dot(match.astype(BF16), before, 1, 0).astype(jnp.int32)
    rank = jnp.where(match > 0.0, rank, -1)
    position = lax.broadcasted_iota(jnp.int32, (owners, CAP, tokens), 1)
    taken = (rank[:, None, :] == position).reshape(slots, tokens)
    weights = jnp.broadcast_to(weight[:, None, :], (owners, CAP, tokens)).reshape(slots, tokens)
    blend = jnp.where(taken, weights, 0.0)
    place = jnp.where(taken, 1.0, 0.0).astype(BF16)
    place_ref[...] = place
    blend_ref[...] = blend.astype(BF16)
    slot_weight = jnp.sum(blend, axis=1, keepdims=True)
    copies[2].wait()
    slot_scale = dot(place, scales_ref[...], 1, 1)
    copies[3].wait()
    codes = dot(place, codes_ref[...], 1, 0)
    features = codes.shape[1]
    groups = scales_ref.shape[0]
    width = features // groups
    rows = jnp.concatenate(
        [codes[:, g * width : (g + 1) * width] * slot_scale[:, g : g + 1] for g in range(groups)],
        axis=1,
    )
    copies[4].wait()
    grads = dot(place, grad_ref[...], 1, 0) * slot_weight
    store_pairs(rows, grads, mine_ref, theirs_ref)


def store_pairs(first, second, mine_ref, theirs_ref):
    chips, _, features = mine_ref.shape
    both = jnp.concatenate(
        [
            first.reshape(chips, CORES, CAP, features),
            second.reshape(chips, CORES, CAP, features),
        ],
        axis=2,
    ).astype(BF16)
    mine_ref[...] = both[:, 0]
    theirs_ref[...] = both[:, 1]


def pack_kernel(mine_ref, got_ref, *outs):
    for k, out in enumerate(outs):
        out[0] = mine_ref[k]
        out[1] = got_ref[k]


def fetch_kernel(
    after_hbm, gate_hbm, up_hbm, down_hbm, gate_ref, up_ref, down_ref, flipped_ref, sems
):
    copies = load_all((down_hbm, gate_hbm, up_hbm), (down_ref, gate_ref, up_ref), sems)
    copies[0].wait()
    flipped_ref[...] = down_ref[...].T
    copies[1].wait()
    copies[2].wait()


def flip_kernel(after_hbm, gate_ref, up_ref, gate_out, up_out):
    gate_out[...] = gate_ref[...].T
    up_out[...] = up_ref[...].T


def unpack(blocks):
    count, _, features = blocks.shape
    wide = blocks.astype(F32).reshape(count, 2, CAP, features)
    return (
        wide[:, 0].reshape(count * CAP, features).astype(BF16),
        wide[:, 1].reshape(count * CAP, features).astype(BF16),
    )


def partial_kernel(*refs, shares):
    blocks_ref = refs[-1]
    sends = refs[-1 - shares - 2 : -3]
    rows_ref, grads_ref = refs[-3:-1]
    gate_ref, up_ref, down_ref = refs[-1 - shares - 5 : -1 - shares - 2]
    got = sort_back(refs[: -1 - shares - 5])
    for k, ref in enumerate(got):
        blocks_ref[CORES * k : CORES * k + CORES] = ref[...]
    owners = blocks_ref.shape[0]
    step = owners // shares
    rows, grads = unpack(
        jnp.concatenate([blocks_ref[pl.ds(peer(shares, s) * step, step)] for s in range(shares)], axis=0)
    )
    rows_ref[...] = rows
    grads_ref[...] = grads
    share = step * CAP
    for i, part in enumerate(
        (
            dot(rows, gate_ref[...], 1, 0),
            dot(rows, up_ref[...], 1, 0),
            dot(grads, down_ref[...], 1, 0),
        )
    ):
        for s, send in enumerate(sends):
            send[i] = part[s * share : (s + 1) * share].astype(BF16)


def gating_kernel(*refs):
    parts, out_ref = refs[:-1], refs[-1]
    gate, up, hidden_grad = (sum(part[i].astype(F32) for part in parts) for i in range(3))
    sig = jax.nn.sigmoid(gate)
    silu = gate * sig
    out_ref[0] = (silu * up).astype(BF16)
    out_ref[1] = (hidden_grad * up * sig * (1.0 + gate * (1.0 - sig))).astype(BF16)
    out_ref[2] = (hidden_grad * silu).astype(BF16)


def output_kernel(*refs):
    (gate_ref, up_ref, down_ref), refs, blocks_ref = refs[:3], refs[3:-1], refs[-1]
    owners, _, features = blocks_ref.shape
    chips = owners // CORES
    acts, sends = sort_back(refs[:-chips]), refs[-chips:]
    shares = len(acts)
    step = owners // shares
    hidden, gate_grad, up_grad = (jnp.concatenate([a[i] for a in acts], axis=0) for i in range(3))
    out = dot(hidden, down_ref[...], 1, 0)
    back = dot(gate_grad, gate_ref[...], 1, 0) + dot(up_grad, up_ref[...], 1, 0)
    both = jnp.concatenate(
        [out.reshape(owners, CAP, features), back.reshape(owners, CAP, features)], axis=1
    ).astype(BF16)
    for s in range(shares):
        blocks_ref[pl.ds(peer(shares, s) * step, step)] = both[s * step : (s + 1) * step]
    for k, send in enumerate(sends):
        send[...] = blocks_ref[CORES * k : CORES * k + CORES]


def pass_kernel(*refs):
    direct, out_ref = refs[1:-1], refs[-1]
    for k, ref in enumerate(sort_back(direct)):
        out_ref[k] = ref[1]


def stream_products(products, sems):
    copies = []
    for i, (left, right, out_ref, out_hbm, first, last) in enumerate(products):
        for j in range(first, last):
            part = slice(j * TILE, (j + 1) * TILE)
            out_ref[part] = dot(left[:, part], right, 0, 0).astype(BF16)
            copy = pltpu.make_async_copy(out_ref.at[part], out_hbm.at[0, part], sems.at[i, j])
            copy.start()
            copies.append(copy)
    for copy in copies:
        copy.wait()


def weight_kernel(*refs):
    (rows_ref, grads_ref), acts = refs[:2], sort_back(refs[2:-8])
    gate_hbm, up_hbm, down_hbm, done_ref, gate_ref, up_ref, down_ref, sems = refs[-8:]
    done_ref[...] = jnp.zeros_like(done_ref)
    rows, grads = rows_ref[...], grads_ref[...]
    hidden, gate_grad, up_grad = (jnp.concatenate([a[i] for a in acts], axis=0) for i in range(3))
    tiles = gate_ref.shape[0] // TILE
    stream_products(
        (
            (rows, gate_grad, gate_ref, gate_hbm, 0, tiles),
            (rows, up_grad, up_ref, up_hbm, 0, tiles),
            (hidden, grads, down_ref, down_hbm, 0, EARLY),
        ),
        sems,
    )


def down_kernel(*refs):
    grads_ref, acts = refs[2], sort_back(refs[3:-3])
    down_hbm, down_ref, sems = refs[-3:]
    hidden = jnp.concatenate([a[0] for a in acts], axis=0)
    last = down_ref.shape[0] // TILE
    stream_products(((hidden, grads_ref[...], down_ref, down_hbm, EARLY, last),), sems)


def combine_kernel(*refs):
    direct, (passed_ref, place_ref, blend_ref, mixed_ref, rows_ref) = refs[:-5], refs[-5:]
    blocks = []
    for k, ref in enumerate(sort_back(direct)):
        blocks += [ref[0], passed_ref[k]]
    outs, backs = unpack(jnp.stack(blocks, axis=0))
    mixed_ref[...] = dot(blend_ref[...], outs, 0, 0).astype(BF16)
    rows_ref[...] = dot(place_ref[...], backs, 0, 0).astype(BF16)


def most_bits_first(count):
    return sorted(range(count), key=lambda k: (k > 0, -k.bit_count(), k))


def sort_back(refs):
    order = most_bits_first(len(refs))
    return [refs[order.index(k)] for k in range(len(refs))]


def trade(array, axis, distance):
    count = lax.axis_size(axis)
    return lax.ppermute(array, axis, [(i, i ^ distance) for i in range(count)])


def trade_dp(array, s):
    shares, owners = lax.axis_size("dp"), lax.axis_size("expert")
    pairs = [
        (d * owners + e, (d ^ distances(shares, e % CORES)[s]) * owners + e)
        for d in range(shares)
        for e in range(owners)
    ]
    return lax.ppermute(array, ("dp", "expert"), pairs)


def swap(mine, theirs):
    chips, rows, features = mine.shape
    got = trade(theirs, "expert", 1)
    packed = call(
        pack_kernel, (jax.ShapeDtypeStruct((CORES, rows, features), BF16),) * chips
    )(mine, got)
    return [trade(packed[k], "expert", CORES * k) if k else packed[0] for k in most_bits_first(chips)]


def on_device(row_codes, scales, routes, mix_weights, w_gate, w_up, w_down, grad_out):
    owners = lax.axis_size("expert")
    shares = lax.axis_size("dp")
    chips = owners // CORES
    tokens, features = row_codes.shape
    width = w_gate.shape[2]
    slots = owners * CAP
    share = slots // shares
    shape = jax.ShapeDtypeStruct
    one = 2 * slots * features * width
    half = shape((chips, 2 * CAP, features), BF16)
    blocks = pltpu.VMEM((owners, 2 * CAP, features), BF16)
    loads = tuple(
        in_hbm(x) for x in (routes.T, mix_weights.T, scales.T, row_codes, grad_out)
    )
    mine, theirs, place, blend = call(
        route_kernel,
        (half, half, shape((slots, tokens), BF16), shape((slots, tokens), BF16)),
        in_specs=[HBM_SPEC] * 5,
        scratch=[pltpu.VMEM(x.shape, x.dtype) for x in loads] + [pltpu.SemaphoreType.DMA((5,))],
    )(*loads)
    got = swap(mine, theirs)
    weights = tuple(in_hbm(w[0]) for w in (w_gate, w_up, w_down))
    weights = call(
        fetch_kernel,
        tuple(pltpu.VMEM(w.shape, w.dtype) for w in weights)
        + (pltpu.VMEM((features, width), BF16),),
        in_specs=[HBM_SPEC] * 4,
        scratch=[pltpu.SemaphoreType.DMA((3,))],
        bytes_accessed=6 * features * width,
    )(got[0], *weights)
    *partials, rows, grads = call(
        lambda *refs: partial_kernel(*refs, shares=shares),
        (shape((3, share, width), BF16),) * shares + (shape((slots, features), BF16),) * 2,
        scratch=[blocks],
        flops=3 * one,
    )(*got, *weights[:2], weights[3])
    gate_w, up_w, down_w, _ = weights
    flipped = call(
        flip_kernel,
        (pltpu.VMEM((width, features), BF16),) * 2,
        in_specs=[HBM_SPEC, VMEM_SPEC, VMEM_SPEC],
        bytes_accessed=16 * features * width,
    )(partials[0], gate_w, up_w)
    summed = [trade_dp(partials[s], s) if s else partials[0] for s in range(shares)]
    act = call(gating_kernel, shape((3, share, width), BF16))(*summed)
    acts = [trade_dp(act, s) if s else act for s in most_bits_first(shares)]
    outs = call(
        output_kernel,
        (shape((CORES, 2 * CAP, features), BF16),) * chips,
        scratch=[blocks],
        flops=3 * one,
    )(*flipped, down_w, *acts)
    back = [
        trade(outs[k], "expert", CORES * k) if k else outs[0] for k in most_bits_first(chips)
    ]
    grad_gate, grad_up, grad_down, done = call(
        weight_kernel,
        (
            shape((1, features, width), BF16),
            shape((1, features, width), BF16),
            shape((1, width, features), BF16),
            pltpu.VMEM((8, 128), F32),
        ),
        out_specs=[HBM_SPEC] * 3 + [VMEM_SPEC],
        scratch=[
            pltpu.VMEM((features, width), BF16),
            pltpu.VMEM((features, width), BF16),
            pltpu.VMEM((width, features), BF16),
            pltpu.SemaphoreType.DMA((3, max(features, width) // TILE)),
        ],
        flops=3 * one,
        bytes_accessed=6 * features * width,
        mib=16,
    )(rows, grads, *acts)
    passed = call(
        pass_kernel,
        shape((chips, 2 * CAP, features), BF16),
        in_specs=[VMEM_SPEC] * (chips + 1),
    )(done, *back)
    any_spec = pl.BlockSpec(memory_space=pl.ANY)
    grad_down = call(
        down_kernel,
        shape((1, width, features), BF16),
        in_specs=[any_spec] * 2 + [VMEM_SPEC] * (shares + 1),
        out_specs=any_spec,
        scratch=[
            pltpu.VMEM((width, features), BF16),
            pltpu.SemaphoreType.DMA((1, width // TILE)),
        ],
        flops=one // 2,
        bytes_accessed=features * width,
        aliases={0: 0},
    )(grad_down, passed, grads, *acts)
    mixed_out, grad_rows = call(
        combine_kernel, (shape((tokens, features), BF16), shape((tokens, features), BF16))
    )(*back, trade(passed, "expert", 1), place, blend)
    return mixed_out, grad_rows, grad_gate, grad_up, grad_down


def solution(mesh):
    placed = (
        P("expert", "dp"),
        P("expert", "dp"),
        P("expert", None),
        P("expert", None),
        P("expert", "dp", None),
        P("expert", "dp", None),
        P("expert", None, "dp"),
        P("expert", "dp"),
    )
    return jax.shard_map(
        on_device,
        mesh=mesh,
        in_specs=placed,
        out_specs=(
            P("expert", "dp"),
            P("expert", "dp"),
            P("expert", "dp", None),
            P("expert", "dp", None),
            P("expert", None, "dp"),
        ),
        check_vma=False,
    )
```
